32 devices in a mesh: sys: 2 (over y), row: 4 (over x, core), col: 4 (over z).
Axes of the slice: x: 2, y: 2, z: 4, core: 2. Of those that a mesh axis runs over, the one named last changes fastest.
Arguments:
- hamiltonian: bfloat16 [2048, 2048], P(('sys', 'row'), 'col'), parts along dimension 0, may hold values from -140 to 140
- row_ids: int32 [8, 4, 4], P(('sys', 'row'), 'col'), parts along dimension 0, may hold values from 0 to 7, as said below
- col_ids: int32 [8, 4, 8], P(('sys', 'row'), 'col'), parts along dimension 0, may hold values from 0 to 7, as said below
- counts: int32 [8, 4, 2], P(('sys', 'row'), 'col'), parts along dimension 0, may hold values from 2 to 8, as said below
Outputs:
- sign_estimate: bfloat16 [2048, 2048], P(('sys', 'row'), 'col'), parts along dimension 0
The draws below stay inside these ranges and needn't reach their ends.
There are 2 independent parts, one for each index of `sys`. The reference program is written for one: setup_inputs(seed, part) draws one part's arguments, and reference() takes and returns one part's arrays. A program takes and returns all parts, laid end to end along the dimension named above; each array names one. Nothing has to cross between parts.
Inputs may be any that keep to these rules, and one draw needn't show every extreme that they name: `row_ids`: within a tile the 4 row ids are distinct. `col_ids`: within a tile the 8 column ids are distinct. counts[i, j, 0] is at most 4 and counts[i, j, 1] at most 8; one tile has both at their most.
All inputs are finite; a program needn't handle non-finite values.
Results may differ from the reference program's by a relative error of at most 0.0057.
Values may be sent and summed in bfloat16 or wider, within the bound.
A program may use at most 64 MiB of HBM per device.

```python
import math
import jax
import jax.numpy as jnp
from jax import lax

BLK = 64
ACT = 8
RT = 4
CT = 8
NS_STEPS = 2
SUB = 1
N_ROW = 4
N_COL = 4


onsite_level = 40.0


offdiag_spread = 0.35


noise_share = 0.5


def block_rows(key):
    key = jax.random.fold_in(key, 8)
    subkeys = jax.random.split(key, N_ROW * N_COL)
    picks = jax.vmap(lambda subkey: jax.random.permutation(subkey, ACT)[:RT])(subkeys)
    return picks.reshape(N_ROW, N_COL, RT).astype(jnp.int32)


def block_cols(key):
    key = jax.random.fold_in(key, 9)
    subkeys = jax.random.split(key, N_ROW * N_COL)
    picks = jax.vmap(lambda subkey: jax.random.permutation(subkey, SUB * ACT)[:CT])(subkeys)
    return picks.reshape(N_ROW, N_COL, CT).astype(jnp.int32)


def draw_hamiltonian(key, part):
    slot_rows = block_rows(key)
    slot_cols = block_cols(key)
    key = jax.random.fold_in(key, 7)
    keys = jax.random.split(key, 9)
    total_rows = N_ROW * RT * BLK
    total_cols = N_COL * CT * BLK
    block_total = N_ROW * ACT
    base = jnp.clip(jax.random.normal(keys[0], (total_rows, total_cols), jnp.float32), -3.0, 3.0)
    base_var = 0.973
    onsite = jnp.exp(jax.random.uniform(keys[5], (block_total, BLK), jnp.float32, math.log(0.5), math.log(1.1)))
    onsite_square = (1.1 ** 2 - 0.5 ** 2) / (2.0 * math.log(2.2))
    row_scale = jnp.exp(jax.random.uniform(keys[1], (total_rows, 1), jnp.float32, 0.0, 1.2))
    col_scale = jnp.exp(jax.random.uniform(keys[2], (1, total_cols), jnp.float32, 0.0, 1.2))
    tile_amp = jnp.exp(jax.random.uniform(keys[4], (N_ROW, N_COL), jnp.float32, -1.0, 1.0))
    ramp_span = max(N_ROW - 1, 1)
    tile_row = (jnp.arange(total_rows) // (RT * BLK)).astype(jnp.float32)
    rising = 1.0 + 2.0 * tile_row / ramp_span
    ramp_square = sum(((1.0 + 2.0 * index / ramp_span) ** 2 for index in range(N_ROW))) / N_ROW
    scale_square = ((math.exp(2.4) - 1.0) / 2.4) ** 2
    amp_square = math.sinh(2.0) / 2.0
    noise_unit = base_var * scale_square * ramp_square * amp_square
    live_cols = (max(CT // 2, 1) + CT) / 2.0
    diag_chance = live_cols / (SUB * ACT) / N_COL
    block_square = (1.25 ** 2 - 0.8 ** 2) / (2.0 * math.log(1.25 / 0.8))
    diag_energy = onsite_level ** 2 * block_square * (onsite_square + offdiag_spread ** 2)
    noise_gain = math.sqrt(diag_chance * diag_energy * noise_share / (1.0 - noise_share) / (live_cols * BLK * noise_unit))
    noise = base * row_scale * col_scale * rising[:, None]
    noise = noise.reshape(N_ROW, RT * BLK, N_COL, CT * BLK) * tile_amp[:, None, :, None] * noise_gain
    block_amp = jnp.exp(jax.random.uniform(keys[6], (block_total,), jnp.float32, math.log(0.8), math.log(1.25)))
    block_sign = (jax.random.randint(keys[7], (block_total,), 0, 2) * 2 - 1).astype(jnp.float32)
    raw = jnp.clip(jax.random.normal(keys[8], (block_total, BLK, BLK), jnp.float32), -3.0, 3.0)
    symmetric = (raw + raw.transpose(0, 2, 1)) / math.sqrt(2.0)
    identity = jnp.eye(BLK, dtype=jnp.float32)
    blocks = identity[None, :, :] * onsite[:, :, None] + offdiag_spread / math.sqrt(BLK) * symmetric
    blocks = blocks * (onsite_level * block_amp * block_sign)[:, None, None]
    global_rows = (jnp.arange(N_ROW)[:, None, None] * ACT + slot_rows).astype(jnp.int32)
    global_cols = (jnp.arange(N_COL)[None, :, None] * (SUB * ACT) + slot_cols).astype(jnp.int32)
    same = (global_rows[:, :, :, None] == global_cols[:, :, None, :]).astype(jnp.float32)
    picked = jnp.take(blocks, global_rows, axis=0)
    onsite_tiles = same[:, :, :, :, None, None] * picked[:, :, :, None, :, :]
    onsite_tiles = onsite_tiles.transpose(0, 2, 4, 1, 3, 5).reshape(N_ROW, RT * BLK, N_COL, CT * BLK)
    value = jnp.clip(noise + onsite_tiles, -140.0, 140.0)
    return value.reshape(total_rows, total_cols).astype(jnp.bfloat16)


def draw_row_ids(key, part):
    shared = block_rows(key)
    return shared


def draw_col_ids(key, part):
    shared = block_cols(key)
    return shared


def draw_counts(key, part):
    key = jax.random.fold_in(key, 10)
    key_rows, key_cols, key_full = jax.random.split(key, 3)
    live_rows = jax.random.randint(key_rows, (N_ROW, N_COL), max(RT // 2, 1), RT + 1)
    live_cols = jax.random.randint(key_cols, (N_ROW, N_COL), max(CT // 2, 1), CT + 1)
    chosen = jax.random.randint(key_full, (), 0, N_ROW * N_COL)
    full_tile = jnp.arange(N_ROW * N_COL).reshape(N_ROW, N_COL) == chosen
    live_rows = jnp.where(full_tile, RT, live_rows)
    live_cols = jnp.where(full_tile, CT, live_cols)
    return jnp.stack([live_rows, live_cols], axis=-1).astype(jnp.int32)


def setup_inputs(seed: int = 0, part: int = 0) -> dict:
    seeds = jax.random.split(jax.random.key(seed), 5)
    part_keys = jax.random.split(jax.random.fold_in(seeds[4], part), 5)
    return {
        "hamiltonian": draw_hamiltonian(jax.random.fold_in(jax.random.fold_in(seeds[4], part), 71), part),
        "row_ids": draw_row_ids(jax.random.fold_in(jax.random.fold_in(seeds[4], part), 71), part),
        "col_ids": draw_col_ids(jax.random.fold_in(jax.random.fold_in(seeds[4], part), 71), part),
        "counts": draw_counts(jax.random.fold_in(jax.random.fold_in(seeds[4], part), 71), part),
    }


def tile_view(whole):
    return whole.reshape(N_ROW, RT * BLK, N_COL, CT * BLK).transpose(0, 2, 1, 3)

def reference(hamiltonian, row_ids, col_ids, counts):
    row_live = jnp.arange(RT)[None, None, :] < counts[:, :, 0:1]
    col_live = jnp.arange(CT)[None, None, :] < counts[:, :, 1:2]
    global_rows = (jnp.arange(N_ROW)[:, None, None] * ACT + row_ids).astype(jnp.int32)
    global_cols = (jnp.arange(N_COL)[None, :, None] * (SUB * ACT) + col_ids).astype(jnp.int32)
    row_mask = jnp.repeat(row_live, BLK, axis=2).astype(jnp.float32)
    col_mask = jnp.repeat(col_live, BLK, axis=2).astype(jnp.float32)
    tile_mask = row_mask[:, :, :, None] * col_mask[:, :, None, :]
    energy = tile_view(hamiltonian).astype(jnp.float32) * tile_mask
    total = jnp.sum(energy * energy)
    live_rows = BLK * jnp.sum(counts[:, :, 0]).astype(jnp.float32)
    scale = 2.0 * jnp.sqrt(N_COL * total / live_rows + 1e-06)
    current = (energy / scale).astype(jnp.bfloat16)
    pair_tile = (jnp.arange(N_ROW) // SUB).astype(jnp.int32)

    def multiply(left, right):

        def one_tile(index):
            row_index = index // N_COL
            col_index = index % N_COL
            own_rows = row_ids[row_index, col_index]
            own_cols = col_ids[row_index, col_index]
            own_row_live = row_live[row_index, col_index]
            own_col_live = col_live[row_index, col_index]
            row_select = (row_ids[row_index][:, None, :] == own_rows[None, :, None]) & row_live[row_index][:, None, :] & own_row_live[None, :, None]
            a_cols = global_cols[row_index][pair_tile]
            a_live = col_live[row_index][pair_tile]
            pair_select = (a_cols[:, None, :] == global_rows[:, col_index][:, :, None]) & a_live[:, None, :] & row_live[:, col_index][:, :, None]
            col_select = (col_ids[:, col_index][:, :, None] == own_cols[None, None, :]) & col_live[:, col_index][:, :, None] & own_col_live[None, None, :]
            a_tiles = left[row_index].astype(jnp.float32).reshape(N_COL, RT, BLK, CT, BLK)
            a_full = jnp.einsum('mca,maxdy->cxmdy', row_select.astype(jnp.float32), a_tiles)
            a_pair = a_full[:, :, pair_tile]
            gathered = jnp.einsum('cxkdy,krd->cxkry', a_pair, pair_select.astype(jnp.float32))
            b_tiles = right[:, col_index].astype(jnp.float32).reshape(N_ROW, RT, BLK, CT, BLK)
            moved = jnp.einsum('krybw,kbq->kryqw', b_tiles, col_select.astype(jnp.float32))
            result = jnp.einsum('cxkry,kryqw->cxqw', gathered, moved)
            return result.reshape(RT * BLK, CT * BLK)
        tiles = lax.map(one_tile, jnp.arange(N_ROW * N_COL, dtype=jnp.int32))
        return tiles.reshape(N_ROW, N_COL, RT * BLK, CT * BLK)
    final = None
    for sweep in range(NS_STEPS):
        square = multiply(current, current).astype(jnp.bfloat16)
        cube = multiply(current, square)
        update = 1.5 * current.astype(jnp.float32) - 0.5 * cube
        if sweep + 1 < NS_STEPS:
            current = update.astype(jnp.bfloat16)
        else:
            final = update * scale
    return final.transpose(0, 2, 1, 3).reshape(N_ROW * RT * BLK, N_COL * CT * BLK).astype(jnp.bfloat16)
```

```python
import jax
import jax.numpy as jnp
from jax import lax
from jax.experimental import pallas as pl
from jax.experimental.pallas import tpu as pltpu
from jax.sharding import PartitionSpec as P

BLK = 64
ACT = 8
RT = 4
CT = 8
NS_STEPS = 2

LINE = 4
ROWS = RT * BLK
COLS = CT * BLK
FULL = LINE * ROWS
MESH_IDS = pl.DeviceIdType.MESH


def onehot(found):
    return jnp.where(found, 1.0, 0.0).astype(jnp.bfloat16)


def dot(a, b):
    return jnp.dot(a, b, preferred_element_type=jnp.float32)


def lines_kernel(
    h_ref, rid, cid, cnt, o_ref,
    tiles, meta, down, left, right, picked, select, masks, half, whole, left2, square2,
    send, recv, meta_send, meta_recv,
):
    k = lax.axis_index("row")
    z = lax.axis_index("col")
    ks = k + 1 - 2 * (k % 2)
    kx = (k + 2) % LINE
    kxs = (ks + 2) % LINE
    barrier = pltpu.get_barrier_semaphore()
    others = [(a, b) for a in range(LINE) for b in range(LINE) if a or b]
    for a, b in others:
        pl.semaphore_signal(
            barrier, inc=1, device_id={"row": (k + a) % LINE, "col": (z + b) % LINE}, device_id_type=MESH_IDS
        )
    live_rows = cnt[0, 0, 0]
    live_cols = cnt[0, 0, 1]

    lane = lax.broadcasted_iota(jnp.int32, (BLK, COLS), 1)
    sub = lax.broadcasted_iota(jnp.int32, (BLK, COLS), 0)
    for c in range(CT):
        offset = jnp.where(c < live_cols, cid[0, 0, c] * BLK, -COLS)
        select[pl.ds(c * BLK, BLK), 0:COLS] = onehot(sub + offset == lane)
    natural = dot(h_ref[...], select[:, 0:COLS])
    energy = jnp.zeros((1, COLS), jnp.float32)
    for r in range(RT):
        part = natural[r * BLK:(r + 1) * BLK] * jnp.where(r < live_rows, 1.0, 0.0)
        tiles[z, pl.ds(pl.multiple_of(k * ROWS + r * BLK, BLK), BLK), :] = part.astype(jnp.bfloat16)
        energy += jnp.sum(part * part, axis=0, keepdims=True)
    lane1 = lax.broadcasted_iota(jnp.int32, (1, COLS), 1)
    block1 = lane1 // BLK
    within = lane1 % BLK
    row_full = jnp.full((1, COLS), -1, jnp.int32)
    for r in range(RT):
        row_full = jnp.where((block1 == r) & (r < live_rows), rid[0, 0, r] * BLK + within, row_full)
    row_full = row_full.astype(jnp.float32)
    col_mask = jnp.zeros((1, COLS), jnp.float32)
    col_full = jnp.full((1, COLS), -1, jnp.int32)
    for c in range(CT):
        alive = c < live_cols
        col_mask = jnp.where((block1 == cid[0, 0, c]) & alive, 1.0, col_mask)
        col_full = jnp.where((block1 == c) & alive, cid[0, 0, c] * BLK + within, col_full)
    own_meta = meta.at[k, z]
    own_meta[0:1, :] = row_full[:, 0:128]
    own_meta[1:2, :] = row_full[:, 128:256]
    for q in range(4):
        own_meta[2 + q:3 + q, :] = col_mask[:, q * 128:(q + 1) * 128]
    own_meta[6:7, :] = energy[:, 0:128] + energy[:, 128:256] + energy[:, 256:384] + energy[:, 384:512]
    own_meta[7:8, :] = jnp.full((1, 128), live_rows, jnp.int32).astype(jnp.float32)
    pl.semaphore_wait(barrier, len(others))

    def piece(kk, m):
        return tiles.at[m, pl.ds(pl.multiple_of(kk * ROWS, ROWS), ROWS), :]

    def copy(kind, kk, m, row, col):
        return pltpu.make_async_remote_copy(
            src_ref=piece(kk, m), dst_ref=piece(kk, m),
            send_sem=send.at[kind, m], recv_sem=recv.at[kk, m],
            device_id={"row": row, "col": col}, device_id_type=MESH_IDS,
        )

    def meta_copy(n, a, b):
        return pltpu.make_async_remote_copy(
            src_ref=meta.at[k, z], dst_ref=meta.at[k, z],
            send_sem=meta_send.at[n], recv_sem=meta_recv.at[k, z],
            device_id={"row": (k + a) % LINE, "col": (z + b) % LINE}, device_id_type=MESH_IDS,
        )

    def line_copies(m, act):
        @pl.when((m <= z) & (z < LINE - 1))
        def _():
            act(copy(0, k, m, k, z + 1))

        @pl.when((m >= z) & (z > 0))
        def _():
            act(copy(1, k, m, k, z - 1))

        act(copy(2, k, m, kx, z))
        act(copy(3, k, m, ks, z))

    def start(c):
        c.start()

    def finish(c):
        c.wait_send()

    def arrived(kk, m):
        copy(0, kk, m, ks, z).wait_recv()

    high = z // 2
    near = z * (1 - high) + (LINE - 1 - z) * high

    def panel_at(t):
        later = t // 2
        m = 2 * later + (t + near * (1 - later)) % 2
        return m * (1 - high) + (LINE - 1 - m) * high

    line_copies(z, start)
    for n, (a, b) in enumerate(others):
        meta_copy(n, a, b).start()
    for a, b in others:
        row, col = (k + a) % LINE, (z + b) % LINE
        pltpu.make_async_remote_copy(
            src_ref=meta.at[row, col], dst_ref=meta.at[row, col],
            send_sem=meta_send.at[0], recv_sem=meta_recv.at[row, col],
            device_id={"row": row, "col": col}, device_id_type=MESH_IDS,
        ).wait_recv()

    def lane_ids(kk, m):
        return jnp.concatenate([meta[kk, m, 0:1, :], meta[kk, m, 1:2, :]], axis=1)

    def natural_mask(kk, m):
        return jnp.concatenate([meta[kk, m, 2 + q:3 + q, :] for q in range(4)], axis=1)

    for a in range(LINE):
        for b in range(LINE):
            for q in range(2):
                wide = jnp.broadcast_to(meta[a, b, q:q + 1, :], (128, 128))
                down[a, b, pl.ds(q * 128, 128), :] = wide.T

    def row_select(kk, to, of):
        ids = down[kk, to]
        return onehot(jnp.concatenate([ids, ids], axis=1) == lane_ids(kk, of))

    sub_wide = lax.broadcasted_iota(jnp.int32, (COLS, ROWS), 0).astype(jnp.float32)

    def col_select(m, to):
        return onehot(sub_wide == lane_ids(m, to))

    def wide_slice(index):
        return pl.ds(pl.multiple_of(index * ROWS, ROWS), ROWS)

    def stage(t, carry):
        @pl.when(t < LINE - 1)
        def _():
            m1 = panel_at(t + 1)
            arrived(k, m1)
            line_copies(m1, start)

        m = panel_at(t)
        arrived(kx, m)
        copy(4, kx, m, ks, z).start()
        for to in range(LINE):
            select[:, pl.ds(to * ROWS, ROWS)] = col_select(m, to)
        arrived(ks, m)
        arrived(kxs, m)

        def rows_of(kk, carry):
            picked[...] = dot(tiles[m, wide_slice(kk), :], select[...]).astype(jnp.bfloat16)
            right[m, wide_slice(kk), :] = picked[:, wide_slice(z)]
            mask = jnp.broadcast_to(natural_mask(kk, m), (16, COLS)).astype(jnp.bfloat16)
            masks[kk, m] = dot(mask, select[:, wide_slice(z)])
            for to in range(LINE):
                block = dot(row_select(kk, to, m), picked[:, pl.ds(to * ROWS, ROWS)])
                left[to, wide_slice(kk), wide_slice(m)] = block.astype(jnp.bfloat16)
            return carry

        return lax.fori_loop(0, LINE, rows_of, carry)

    lax.fori_loop(0, LINE, stage, 0)

    total = jnp.zeros((1, 128), jnp.float32)
    count = jnp.zeros((1, 128), jnp.float32)
    for a in range(LINE):
        for b in range(LINE):
            total += meta[a, b, 6:7, :]
            count += meta[a, b, 7:8, :]
    total = jnp.sum(total, axis=1, keepdims=True)
    count = jnp.max(count, axis=1, keepdims=True) * BLK
    scale = 2.0 * jnp.sqrt(LINE * total / count + 1e-06)
    lin = 1.5 / scale
    cub = 0.5 / scale / scale / scale

    def other(d, carry):
        m = (z + d) % LINE

        def square_rows(kk, carry):
            part = dot(left[m, wide_slice(kk), :], right[m]) * masks[kk, m, 0:1, :]
            half[wide_slice(kk), :] = part.astype(jnp.bfloat16)
            return carry

        lax.fori_loop(0, LINE, square_rows, 0)

        def cube_rows(kk, carry):
            part = dot(left[m, wide_slice(kk), :], half[...]) * masks[kk, m, 0:1, :]
            new = lin * right[m, wide_slice(kk), :].astype(jnp.float32) - cub * part
            moved = dot(row_select(kk, z, m), new.astype(jnp.bfloat16))
            left2[wide_slice(kk), wide_slice(m)] = moved.astype(jnp.bfloat16)
            return carry

        return lax.fori_loop(0, LINE, cube_rows, carry)

    lax.fori_loop(1, LINE, other, 0)

    def own_square(kk, carry):
        part = dot(left[z, wide_slice(kk), :], tiles[z]) * natural_mask(kk, z)
        square2[wide_slice(kk), :] = part.astype(jnp.bfloat16)
        return carry

    lax.fori_loop(0, LINE, own_square, 0)
    select[:, 0:ROWS] = col_select(z, z)

    def own_cube(kk, carry):
        part = dot(left[z, wide_slice(kk), :], square2[...]) * natural_mask(kk, z)
        new = lin * tiles[z, wide_slice(kk), :].astype(jnp.float32) - cub * part
        new = new.astype(jnp.bfloat16)
        whole[wide_slice(kk), :] = new
        left2[wide_slice(kk), wide_slice(z)] = dot(new, select[:, 0:ROWS]).astype(jnp.bfloat16)
        return carry

    lax.fori_loop(0, LINE, own_cube, 0)

    def second_square(kk, carry):
        part = dot(left2[wide_slice(kk), :], whole[...]) * natural_mask(kk, z)
        square2[wide_slice(kk), :] = part.astype(jnp.bfloat16)
        return carry

    lax.fori_loop(0, LINE, second_square, 0)
    cube = dot(left2[wide_slice(k), :], square2[...]) * natural_mask(k, z)
    update = 1.5 * whole[wide_slice(k), :].astype(jnp.float32) - 0.5 * cube
    final = (update * scale).astype(jnp.bfloat16)
    back = onehot(lax.broadcasted_iota(jnp.int32, (COLS, COLS), 0) == col_full)
    o_ref[...] = dot(final, back).astype(jnp.bfloat16)

    for n, (a, b) in enumerate(others):
        meta_copy(n, a, b).wait_send()

    def drain(m, carry):
        line_copies(m, finish)
        copy(4, kx, m, ks, z).wait_send()
        return carry

    lax.fori_loop(0, LINE, drain, 0)


def line_shards(hamiltonian, row_ids, col_ids, counts):
    smem = pl.BlockSpec(memory_space=pltpu.SMEM)
    vmem = pl.BlockSpec(memory_space=pltpu.VMEM)
    bf16, f32 = jnp.bfloat16, jnp.float32
    return pl.pallas_call(
        lines_kernel,
        out_shape=jax.ShapeDtypeStruct((ROWS, COLS), bf16),
        in_specs=[vmem, smem, smem, smem],
        out_specs=vmem,
        scratch_shapes=[
            pltpu.VMEM((LINE, FULL, COLS), bf16),
            pltpu.VMEM((LINE, LINE, 8, 128), f32),
            pltpu.VMEM((LINE, LINE, ROWS, 128), f32),
            pltpu.VMEM((LINE, FULL, FULL), bf16),
            pltpu.VMEM((LINE, FULL, ROWS), bf16),
            pltpu.VMEM((ROWS, FULL), bf16),
            pltpu.VMEM((COLS, FULL), bf16),
            pltpu.VMEM((LINE, LINE, 16, ROWS), f32),
            pltpu.VMEM((FULL, ROWS), bf16),
            pltpu.VMEM((FULL, COLS), bf16),
            pltpu.VMEM((FULL, FULL), bf16),
            pltpu.VMEM((FULL, COLS), bf16),
            pltpu.SemaphoreType.DMA((5, LINE)),
            pltpu.SemaphoreType.DMA((LINE, LINE)),
            pltpu.SemaphoreType.DMA((LINE * LINE - 1,)),
            pltpu.SemaphoreType.DMA((LINE, LINE)),
        ],
        compiler_params=pltpu.CompilerParams(
            collective_id=0, has_side_effects=True, vmem_limit_bytes=48 * 1024 * 1024
        ),
        cost_estimate=pl.CostEstimate(flops=13_000_000_000, bytes_accessed=8_000_000, transcendentals=0),
    )(hamiltonian, row_ids, col_ids, counts)


def shards(hamiltonian, row_ids, col_ids, counts):
    grid_rows = lax.axis_size("row")
    grid_cols = lax.axis_size("col")
    sub_panels = grid_rows // grid_cols
    my_row = lax.axis_index("row")
    my_col = lax.axis_index("col")
    tile_rows = hamiltonian.shape[0]
    tile_cols = hamiltonian.shape[1]
    every_rows, every_cols, every_counts = (
        lax.all_gather(row_ids, ("row", "col"), axis=0, tiled=True),
        lax.all_gather(col_ids, ("row", "col"), axis=0, tiled=True),
        lax.all_gather(counts, ("row", "col"), axis=0, tiled=True),
    )
    every_rows = every_rows.reshape(grid_rows, grid_cols, RT)
    every_cols = every_cols.reshape(grid_rows, grid_cols, CT)
    every_counts = every_counts.reshape(grid_rows, grid_cols, 2)
    row_live = jnp.arange(RT)[None, None, :] < every_counts[:, :, 0:1]
    col_live = jnp.arange(CT)[None, None, :] < every_counts[:, :, 1:2]
    global_rows = jnp.arange(grid_rows, dtype=jnp.int32)[:, None, None] * ACT + every_rows
    global_cols = (
        jnp.arange(grid_cols, dtype=jnp.int32)[None, :, None] * (sub_panels * ACT) + every_cols
    )
    own_rows = every_rows[my_row, my_col]
    own_cols = every_cols[my_row, my_col]
    own_row_live = row_live[my_row, my_col]
    own_col_live = col_live[my_row, my_col]
    block_mask = (
        jnp.repeat(own_row_live, BLK)[:, None] & jnp.repeat(own_col_live, BLK)[None, :]
    ).astype(jnp.float32)
    energy = hamiltonian.astype(jnp.float32) * block_mask
    total = lax.psum(jnp.sum(energy * energy), ("row", "col"))
    live_total = BLK * jnp.sum(every_counts[:, :, 0]).astype(jnp.float32)
    scale = 2.0 * jnp.sqrt(grid_cols * total / live_total + 1e-06)
    current = (energy / scale).astype(jnp.bfloat16)
    panel_rows = every_rows[my_row]
    row_match = (
        (panel_rows[:, None, :] == own_rows[None, :, None])
        & row_live[my_row][:, None, :]
        & own_row_live[None, :, None]
    )
    row_select = row_match.astype(jnp.bfloat16)
    pair_tile = jnp.arange(grid_rows, dtype=jnp.int32) // sub_panels
    left_cols = global_cols[my_row][pair_tile]
    left_live = col_live[my_row][pair_tile]
    right_rows = global_rows[:, my_col]
    right_live = row_live[:, my_col]
    matches = (
        (left_cols[:, None, :] == right_rows[:, :, None])
        & left_live[:, None, :]
        & right_live[:, :, None]
    )
    present_pairs = jnp.sum(matches.astype(jnp.int32), axis=2).reshape(-1)
    column_slot = (
        jnp.sum(jnp.where(matches, jnp.arange(CT, dtype=jnp.int32)[None, None, :], 0), axis=2)
        + pair_tile[:, None] * CT
    ).reshape(-1)
    col_match = (
        (every_cols[:, my_col][:, :, None] == own_cols[None, None, :])
        & col_live[:, my_col][:, :, None]
        & own_col_live[None, None, :]
    )
    col_tiles = col_match.astype(jnp.bfloat16)

    def multiply(left_full, right):
        left_blocks = left_full.reshape(tile_rows, grid_cols * CT, BLK)
        piece = lax.all_gather(right, "row", axis=0, tiled=True)
        piece_rows = piece.shape[0]
        tiles = piece_rows // tile_rows
        tile_index = jnp.arange(tiles, dtype=jnp.int32)
        selector = jnp.take(col_tiles, tile_index, axis=0)
        blocks = piece.reshape(tiles, tile_rows, CT, BLK)
        moved = jnp.einsum("tnxw,txc->tncw", blocks, selector, preferred_element_type=jnp.float32)
        moved = moved.astype(jnp.bfloat16).reshape(piece_rows, tile_cols)
        picked = jnp.take(left_blocks, column_slot, axis=1)
        picked = jnp.where(present_pairs[None, :, None] > 0, picked, jnp.zeros_like(picked))
        picked = picked.reshape(tile_rows, piece_rows)
        return jnp.dot(picked, moved, preferred_element_type=jnp.float32)

    final = None
    for sweep in range(NS_STEPS):
        arrange_blocks = lax.all_gather(current, "col", axis=1, tiled=True).reshape(
            RT, BLK, grid_cols, tile_cols
        )
        mapped = jnp.einsum(
            "mca,axmw->cxmw", row_select, arrange_blocks, preferred_element_type=jnp.float32
        )
        left_full = mapped.astype(jnp.bfloat16).reshape(tile_rows, grid_cols * tile_cols)
        square = multiply(left_full, current).astype(jnp.bfloat16)
        cube = multiply(left_full, square)
        update = 1.5 * current.astype(jnp.float32) - 0.5 * cube
        if sweep + 1 < NS_STEPS:
            current = update.astype(jnp.bfloat16)
        else:
            final = (update * scale).astype(jnp.bfloat16)
    return final


def solution(mesh):
    in_specs = (
        P(("sys", "row"), "col"),
        P(("sys", "row"), "col", None),
        P(("sys", "row"), "col", None),
        P(("sys", "row"), "col", None),
    )
    out_specs = P(("sys", "row"), "col")
    small = mesh.shape["row"] == LINE and mesh.shape["col"] == LINE
    return jax.shard_map(line_shards if small else shards, mesh=mesh, in_specs=in_specs, out_specs=out_specs, check_vma=False)
```

```python
import jax
import jax.numpy as jnp
from jax import lax
from jax.experimental import pallas as pl
from jax.experimental.pallas import tpu as pltpu
from jax.sharding import PartitionSpec as P

BLK = 64
ACT = 8
RT = 4
CT = 8
NS_STEPS = 2

LINE = 4
ROWS = RT * BLK
COLS = CT * BLK
FULL = LINE * ROWS
PARTS = 2
PART = ROWS // PARTS
MESH_IDS = pl.DeviceIdType.MESH


def onehot(found):
    return jnp.where(found, 1.0, 0.0).astype(jnp.bfloat16)


def dot(a, b):
    return jnp.dot(a, b, preferred_element_type=jnp.float32)


def lines_kernel(
    h_any, rid_any, cid_any, cnt_any, o_ref,
    h_ref, rid, cid, cnt, tiles, meta, short_ids, ids, left, right, picked, select, masks, half, whole, left2, square2,
    send, recv, meta_send, meta_recv, load,
):
    loads = [
        pltpu.make_async_copy(src, dst, load.at[n])
        for n, (src, dst) in enumerate(((rid_any, rid), (cid_any, cid), (cnt_any, cnt), (h_any, h_ref)))
    ]
    for item in loads:
        item.start()
    k = lax.axis_index("row")
    z = lax.axis_index("col")
    ks = k + 1 - 2 * (k % 2)
    kx = (k + 2) % LINE
    kxs = (ks + 2) % LINE
    barrier = pltpu.get_barrier_semaphore()
    peers = [((k + a) % LINE, z) for a in range(1, LINE)] + [(k, (z + a) % LINE) for a in range(1, LINE)]
    for row, col in peers:
        pl.semaphore_signal(barrier, inc=1, device_id={"row": row, "col": col}, device_id_type=MESH_IDS)
    for item in loads[:3]:
        item.wait()
    live_rows = cnt[0, 0, 0]
    live_cols = cnt[0, 0, 1]

    lane1 = lax.broadcasted_iota(jnp.int32, (1, COLS), 1)
    block1 = lane1 // BLK
    within = lane1 % BLK
    row_full = jnp.full((1, COLS), -1, jnp.int32)
    for r in range(RT):
        row_full = jnp.where((block1 == r) & (r < live_rows), rid[0, 0, r] * BLK + within, row_full)
    col_mask = jnp.zeros((1, COLS), jnp.int32)
    col_full = jnp.full((1, COLS), -1, jnp.int32)
    for c in range(CT):
        alive = c < live_cols
        col_mask = jnp.where((block1 == cid[0, 0, c]) & alive, 1, col_mask)
        col_full = jnp.where((block1 == c) & alive, cid[0, 0, c] * BLK + within, col_full)
    own_meta = meta.at[z, k]
    own_meta[0:1, :] = row_full[:, 0:128]
    own_meta[1:2, :] = row_full[:, 128:256]
    for q in range(4):
        own_meta[2 + q:3 + q, :] = col_mask[:, q * 128:(q + 1) * 128]
    short = jnp.where(lane1[:, 0:128] == RT, live_rows, -1)
    for r in range(RT):
        short = jnp.where((lane1[:, 0:128] == r) & (r < live_rows), rid[0, 0, r], short)
    own_meta[6:7, :] = short
    own_meta[7:8, :] = short
    lane = lax.broadcasted_iota(jnp.int32, (BLK, COLS), 1)
    sub = lax.broadcasted_iota(jnp.int32, (BLK, COLS), 0)
    for c in range(CT):
        offset = jnp.where(c < live_cols, cid[0, 0, c] * BLK, -COLS)
        select[pl.ds(c * BLK, BLK), 0:COLS] = onehot(sub + offset == lane)
    loads[3].wait()
    natural = dot(h_ref[...], select[:, 0:COLS])
    for r in range(RT):
        part = natural[r * BLK:(r + 1) * BLK] * jnp.where(r < live_rows, 1.0, 0.0)
        tiles[z, pl.ds(pl.multiple_of(k * ROWS + r * BLK, BLK), BLK), :] = part.astype(jnp.bfloat16)
    pl.semaphore_wait(barrier, len(peers))

    def piece(kk, m, part):
        return tiles.at[m, pl.ds(pl.multiple_of(kk * ROWS + part * PART, PART), PART), :]

    def copy(kind, kk, m, part, row, col):
        return pltpu.make_async_remote_copy(
            src_ref=piece(kk, m, part), dst_ref=piece(kk, m, part),
            send_sem=send.at[kind, m, part], recv_sem=recv.at[kk, m, part],
            device_id={"row": row, "col": col}, device_id_type=MESH_IDS,
        )

    def row_ids_copy(n, owner, row):
        return pltpu.make_async_remote_copy(
            src_ref=meta.at[z, owner], dst_ref=meta.at[z, owner],
            send_sem=meta_send.at[n], recv_sem=meta_recv.at[0, owner],
            device_id={"row": row, "col": z}, device_id_type=MESH_IDS,
        )

    def line_ids_copy(n, owner, col):
        return pltpu.make_async_remote_copy(
            src_ref=meta.at[owner], dst_ref=meta.at[owner],
            send_sem=meta_send.at[n], recv_sem=meta_recv.at[1, owner],
            device_id={"row": k, "col": col}, device_id_type=MESH_IDS,
        )

    def line_copies(m, part, act):
        @pl.when((m <= z) & (z < LINE - 1))
        def _():
            act(copy(0, k, m, part, k, z + 1))

        @pl.when((m >= z) & (z > 0))
        def _():
            act(copy(1, k, m, part, k, z - 1))

        act(copy(2, k, m, part, kx, z))
        act(copy(3, k, m, part, ks, z))

    def start(c):
        c.start()

    def finish(c):
        c.wait_send()

    def arrived(kk, m, part):
        copy(0, kk, m, part, ks, z).wait_recv()

    high = z // 2
    near = z * (1 - high) + (LINE - 1 - z) * high

    def panel_at(t):
        later = t // 2
        m = 2 * later + (t + near * (1 - later)) % 2
        return m * (1 - high) + (LINE - 1 - m) * high

    for n, (row, _) in enumerate(peers[:3]):
        row_ids_copy(n, k, row).start()
    for part in range(PARTS):
        line_copies(z, part, start)
    for row, _ in peers[:3]:
        row_ids_copy(0, row, row).wait_recv()
    for n, (_, col) in enumerate(peers[3:]):
        line_ids_copy(3 + n, z, col).start()
    for _, col in peers[3:]:
        line_ids_copy(3, col, col).wait_recv()
    for m in range(LINE):
        for kk in range(LINE):
            short_ids[pl.ds(m * LINE + kk, 1), :] = meta[m, kk, 6:7, :]
    spell = pltpu.make_async_copy(short_ids, ids, load.at[4])
    spell.start()
    spell.wait()

    def lane_ids(kk, m):
        return jnp.concatenate([meta[m, kk, 0:1, :], meta[m, kk, 1:2, :]], axis=1)

    def natural_mask(kk, m):
        return jnp.concatenate([meta[m, kk, 2 + q:3 + q, :] for q in range(4)], axis=1).astype(jnp.float32)

    def pick_rows(kk, to, of):
        blocks = []
        for r in range(RT):
            want = ids[to * LINE + kk, r]
            block = jnp.zeros((BLK, ROWS), jnp.bfloat16)
            for a in range(RT):
                same = (ids[of * LINE + kk, a] == want) & (want >= 0)
                block = jnp.where(same, picked[pl.ds(kk * ROWS + a * BLK, BLK), :], block)
            blocks.append(block)
        return jnp.concatenate(blocks, axis=0)

    sub_wide = lax.broadcasted_iota(jnp.int32, (COLS, ROWS), 0)

    def col_select(m, to):
        return onehot(sub_wide == lane_ids(m, to))

    def wide_slice(index):
        return pl.ds(pl.multiple_of(index * ROWS, ROWS), ROWS)

    def stage(t, carry):
        for now, then in ((0, 1), (0, 2), (1, 3)):
            @pl.when(t == now)
            def _(then=then):
                m1 = panel_at(then)
                for part in range(PARTS):
                    arrived(k, m1, part)
                    line_copies(m1, part, start)

        m = panel_at(t)
        for part in range(PARTS):
            arrived(kx, m, part)
            copy(4, kx, m, part, ks, z).start()
        for to in range(LINE):
            select[:, pl.ds(to * ROWS, ROWS)] = col_select(m, to)
        for part in range(PARTS):
            arrived(ks, m, part)
            arrived(kxs, m, part)

        mask = jnp.concatenate(
            [natural_mask(kk, m) for kk in range(LINE)] + [jnp.zeros((12, COLS), jnp.float32)], axis=0
        )
        masks[m] = dot(mask.astype(jnp.bfloat16), select[:, wide_slice(z)])
        for to in range(LINE):
            picked[0:FULL, :] = dot(tiles[m], select[:, pl.ds(to * ROWS, ROWS)]).astype(jnp.bfloat16)

            @pl.when(z == to)
            def _():
                right[m] = picked[0:FULL, :]

            for kk in range(LINE):
                left[to, pl.ds(kk * ROWS, ROWS), wide_slice(m)] = pick_rows(kk, to, m)
        values = tiles[m].astype(jnp.float32)
        return carry + jnp.sum(values * values, axis=0, keepdims=True)

    total = lax.fori_loop(0, LINE, stage, jnp.zeros((1, COLS), jnp.float32))

    total = jnp.sum(total, axis=1, keepdims=True)
    count = jnp.int32(0)
    for a in range(LINE):
        for b in range(LINE):
            count += ids[a * LINE + b, RT]
    count = jnp.full((1, 1), count * BLK, jnp.int32).astype(jnp.float32)
    scale = 2.0 * jnp.sqrt(LINE * total / count + 1e-06)
    lin = 1.5 / scale
    cub = 0.5 / scale / scale / scale

    def spread(rows):
        return jnp.concatenate([jnp.broadcast_to(row, (ROWS, row.shape[1])) for row in rows], axis=0)

    def other(d, carry):
        m = (z + d) % LINE
        mask = spread([masks[m, kk:kk + 1, :] for kk in range(LINE)])
        half[...] = (dot(left[m], right[m]) * mask).astype(jnp.bfloat16)
        part = dot(left[m], half[...]) * mask
        picked[0:FULL, :] = (lin * right[m].astype(jnp.float32) - cub * part).astype(jnp.bfloat16)
        for kk in range(LINE):
            left2[pl.ds(kk * ROWS, ROWS), wide_slice(m)] = pick_rows(kk, z, m)
        return carry

    lax.fori_loop(1, LINE, other, 0)

    mask = spread([natural_mask(kk, z) for kk in range(LINE)])
    square2[...] = (dot(left[z], tiles[z]) * mask).astype(jnp.bfloat16)
    select[:, 0:ROWS] = col_select(z, z)
    part = dot(left[z], square2[...]) * mask
    whole[...] = (lin * tiles[z].astype(jnp.float32) - cub * part).astype(jnp.bfloat16)
    left2[:, wide_slice(z)] = dot(whole[...], select[:, 0:ROWS]).astype(jnp.bfloat16)
    square2[...] = (dot(left2[...], whole[...]) * mask).astype(jnp.bfloat16)
    cube = dot(left2[wide_slice(k), :], square2[...]) * natural_mask(k, z)
    update = 1.5 * whole[wide_slice(k), :].astype(jnp.float32) - 0.5 * cube
    final = (update * scale).astype(jnp.bfloat16)
    back = onehot(lax.broadcasted_iota(jnp.int32, (COLS, COLS), 0) == col_full)
    o_ref[...] = dot(final, back).astype(jnp.bfloat16)

    for n, (row, _) in enumerate(peers[:3]):
        row_ids_copy(n, k, row).wait_send()
    for n, (_, col) in enumerate(peers[3:]):
        line_ids_copy(3 + n, z, col).wait_send()

    def drain(m, carry):
        for part in range(PARTS):
            line_copies(m, part, finish)
            copy(4, kx, m, part, ks, z).wait_send()
        return carry

    lax.fori_loop(0, LINE, drain, 0)


def line_shards(hamiltonian, row_ids, col_ids, counts):
    hbm = pl.BlockSpec(memory_space=pl.ANY)
    vmem = pl.BlockSpec(memory_space=pltpu.VMEM)
    bf16, f32 = jnp.bfloat16, jnp.float32
    return pl.pallas_call(
        lines_kernel,
        out_shape=jax.ShapeDtypeStruct((ROWS, COLS), bf16),
        in_specs=[hbm, hbm, hbm, hbm],
        out_specs=vmem,
        scratch_shapes=[
            pltpu.VMEM((ROWS, COLS), bf16),
            pltpu.SMEM(row_ids.shape, jnp.int32),
            pltpu.SMEM(col_ids.shape, jnp.int32),
            pltpu.SMEM(counts.shape, jnp.int32),
            pltpu.VMEM((LINE, FULL, COLS), bf16),
            pltpu.VMEM((LINE, LINE, 8, 128), jnp.int32),
            pltpu.VMEM((LINE * LINE, 128), jnp.int32),
            pltpu.SMEM((LINE * LINE, 128), jnp.int32),
            pltpu.VMEM((LINE, FULL, FULL), bf16),
            pltpu.VMEM((LINE, FULL, ROWS), bf16),
            pltpu.VMEM((FULL, ROWS), bf16),
            pltpu.VMEM((COLS, FULL), bf16),
            pltpu.VMEM((LINE, 16, ROWS), f32),
            pltpu.VMEM((FULL, ROWS), bf16),
            pltpu.VMEM((FULL, COLS), bf16),
            pltpu.VMEM((FULL, FULL), bf16),
            pltpu.VMEM((FULL, COLS), bf16),
            pltpu.SemaphoreType.DMA((5, LINE, PARTS)),
            pltpu.SemaphoreType.DMA((LINE, LINE, PARTS)),
            pltpu.SemaphoreType.DMA((6,)),
            pltpu.SemaphoreType.DMA((2, LINE)),
            pltpu.SemaphoreType.DMA((5,)),
        ],
        compiler_params=pltpu.CompilerParams(
            collective_id=0, has_side_effects=True, vmem_limit_bytes=48 * 1024 * 1024
        ),
        cost_estimate=pl.CostEstimate(flops=13_000_000_000, bytes_accessed=8_000_000, transcendentals=0),
    )(hamiltonian, row_ids, col_ids, counts)


def shards(hamiltonian, row_ids, col_ids, counts):
    grid_rows = lax.axis_size("row")
    grid_cols = lax.axis_size("col")
    sub_panels = grid_rows // grid_cols
    my_row = lax.axis_index("row")
    my_col = lax.axis_index("col")
    tile_rows = hamiltonian.shape[0]
    tile_cols = hamiltonian.shape[1]
    every_rows, every_cols, every_counts = (
        lax.all_gather(row_ids, ("row", "col"), axis=0, tiled=True),
        lax.all_gather(col_ids, ("row", "col"), axis=0, tiled=True),
        lax.all_gather(counts, ("row", "col"), axis=0, tiled=True),
    )
    every_rows = every_rows.reshape(grid_rows, grid_cols, RT)
    every_cols = every_cols.reshape(grid_rows, grid_cols, CT)
    every_counts = every_counts.reshape(grid_rows, grid_cols, 2)
    row_live = jnp.arange(RT)[None, None, :] < every_counts[:, :, 0:1]
    col_live = jnp.arange(CT)[None, None, :] < every_counts[:, :, 1:2]
    global_rows = jnp.arange(grid_rows, dtype=jnp.int32)[:, None, None] * ACT + every_rows
    global_cols = (
        jnp.arange(grid_cols, dtype=jnp.int32)[None, :, None] * (sub_panels * ACT) + every_cols
    )
    own_rows = every_rows[my_row, my_col]
    own_cols = every_cols[my_row, my_col]
    own_row_live = row_live[my_row, my_col]
    own_col_live = col_live[my_row, my_col]
    block_mask = (
        jnp.repeat(own_row_live, BLK)[:, None] & jnp.repeat(own_col_live, BLK)[None, :]
    ).astype(jnp.float32)
    energy = hamiltonian.astype(jnp.float32) * block_mask
    total = lax.psum(jnp.sum(energy * energy), ("row", "col"))
    live_total = BLK * jnp.sum(every_counts[:, :, 0]).astype(jnp.float32)
    scale = 2.0 * jnp.sqrt(grid_cols * total / live_total + 1e-06)
    current = (energy / scale).astype(jnp.bfloat16)
    panel_rows = every_rows[my_row]
    row_match = (
        (panel_rows[:, None, :] == own_rows[None, :, None])
        & row_live[my_row][:, None, :]
        & own_row_live[None, :, None]
    )
    row_select = row_match.astype(jnp.bfloat16)
    pair_tile = jnp.arange(grid_rows, dtype=jnp.int32) // sub_panels
    left_cols = global_cols[my_row][pair_tile]
    left_live = col_live[my_row][pair_tile]
    right_rows = global_rows[:, my_col]
    right_live = row_live[:, my_col]
    matches = (
        (left_cols[:, None, :] == right_rows[:, :, None])
        & left_live[:, None, :]
        & right_live[:, :, None]
    )
    present_pairs = jnp.sum(matches.astype(jnp.int32), axis=2).reshape(-1)
    column_slot = (
        jnp.sum(jnp.where(matches, jnp.arange(CT, dtype=jnp.int32)[None, None, :], 0), axis=2)
        + pair_tile[:, None] * CT
    ).reshape(-1)
    col_match = (
        (every_cols[:, my_col][:, :, None] == own_cols[None, None, :])
        & col_live[:, my_col][:, :, None]
        & own_col_live[None, None, :]
    )
    col_tiles = col_match.astype(jnp.bfloat16)

    def multiply(left_full, right):
        left_blocks = left_full.reshape(tile_rows, grid_cols * CT, BLK)
        piece = lax.all_gather(right, "row", axis=0, tiled=True)
        piece_rows = piece.shape[0]
        tiles = piece_rows // tile_rows
        tile_index = jnp.arange(tiles, dtype=jnp.int32)
        selector = jnp.take(col_tiles, tile_index, axis=0)
        blocks = piece.reshape(tiles, tile_rows, CT, BLK)
        moved = jnp.einsum("tnxw,txc->tncw", blocks, selector, preferred_element_type=jnp.float32)
        moved = moved.astype(jnp.bfloat16).reshape(piece_rows, tile_cols)
        picked = jnp.take(left_blocks, column_slot, axis=1)
        picked = jnp.where(present_pairs[None, :, None] > 0, picked, jnp.zeros_like(picked))
        picked = picked.reshape(tile_rows, piece_rows)
        return jnp.dot(picked, moved, preferred_element_type=jnp.float32)

    final = None
    for sweep in range(NS_STEPS):
        arrange_blocks = lax.all_gather(current, "col", axis=1, tiled=True).reshape(
            RT, BLK, grid_cols, tile_cols
        )
        mapped = jnp.einsum(
            "mca,axmw->cxmw", row_select, arrange_blocks, preferred_element_type=jnp.float32
        )
        left_full = mapped.astype(jnp.bfloat16).reshape(tile_rows, grid_cols * tile_cols)
        square = multiply(left_full, current).astype(jnp.bfloat16)
        cube = multiply(left_full, square)
        update = 1.5 * current.astype(jnp.float32) - 0.5 * cube
        if sweep + 1 < NS_STEPS:
            current = update.astype(jnp.bfloat16)
        else:
            final = (update * scale).astype(jnp.bfloat16)
    return final


def solution(mesh):
    in_specs = (
        P(("sys", "row"), "col"),
        P(("sys", "row"), "col", None),
        P(("sys", "row"), "col", None),
        P(("sys", "row"), "col", None),
    )
    out_specs = P(("sys", "row"), "col")
    small = mesh.shape["row"] == LINE and mesh.shape["col"] == LINE
    return jax.shard_map(line_shards if small else shards, mesh=mesh, in_specs=in_specs, out_specs=out_specs, check_vma=False)
```

```python
import jax
import jax.numpy as jnp
from jax import lax
from jax.experimental import pallas as pl
from jax.experimental.pallas import tpu as pltpu
from jax.sharding import PartitionSpec as P

BLK = 64
ACT = 8
RT = 4
CT = 8
NS_STEPS = 2

LINE = 4
ROWS = RT * BLK
COLS = CT * BLK
FULL = LINE * ROWS
PARTS = 2
PART = ROWS // PARTS
MESH_IDS = pl.DeviceIdType.MESH


def onehot(found):
    return jnp.where(found, 1.0, 0.0).astype(jnp.bfloat16)


def dot(a, b):
    return jnp.dot(a, b, preferred_element_type=jnp.float32)


def lines_kernel(
    h_any, rid_any, cid_any, cnt_any, o_ref,
    h_ref, rid, cid, cnt, tiles, meta, short_ids, ids, left, right, wide, picked, select, masks, half, whole, left2, square2,
    send, recv, meta_send, meta_recv, load,
):
    loads = [
        pltpu.make_async_copy(src, dst, load.at[n])
        for n, (src, dst) in enumerate(((rid_any, rid), (cid_any, cid), (cnt_any, cnt), (h_any, h_ref)))
    ]
    for item in loads:
        item.start()
    k = lax.axis_index("row")
    z = lax.axis_index("col")
    ks = k + 1 - 2 * (k % 2)
    kx = (k + 2) % LINE
    kxs = (ks + 2) % LINE
    barrier = pltpu.get_barrier_semaphore()
    peers = [((k + a) % LINE, z) for a in range(1, LINE)] + [(k, (z + a) % LINE) for a in range(1, LINE)]
    for row, col in peers:
        pl.semaphore_signal(barrier, inc=1, device_id={"row": row, "col": col}, device_id_type=MESH_IDS)
    for item in loads[:3]:
        item.wait()
    live_rows = cnt[0, 0, 0]
    live_cols = cnt[0, 0, 1]

    lane1 = lax.broadcasted_iota(jnp.int32, (1, COLS), 1)
    block1 = lane1 // BLK
    within = lane1 % BLK
    row_full = jnp.full((1, COLS), -1, jnp.int32)
    for r in range(RT):
        row_full = jnp.where((block1 == r) & (r < live_rows), rid[0, 0, r] * BLK + within, row_full)
    col_mask = jnp.zeros((1, COLS), jnp.int32)
    col_full = jnp.full((1, COLS), -1, jnp.int32)
    for c in range(CT):
        alive = c < live_cols
        col_mask = jnp.where((block1 == cid[0, 0, c]) & alive, 1, col_mask)
        col_full = jnp.where((block1 == c) & alive, cid[0, 0, c] * BLK + within, col_full)
    own_meta = meta.at[z, k]
    own_meta[0:1, :] = row_full[:, 0:128]
    own_meta[1:2, :] = row_full[:, 128:256]
    for q in range(4):
        own_meta[2 + q:3 + q, :] = col_mask[:, q * 128:(q + 1) * 128]
    short = jnp.where(lane1[:, 0:128] == RT, live_rows, -1)
    for r in range(RT):
        short = jnp.where((lane1[:, 0:128] == r) & (r < live_rows), rid[0, 0, r], short)
    own_meta[6:7, :] = short
    own_meta[7:8, :] = short
    lane = lax.broadcasted_iota(jnp.int32, (BLK, COLS), 1)
    sub = lax.broadcasted_iota(jnp.int32, (BLK, COLS), 0)
    for c in range(CT):
        offset = jnp.where(c < live_cols, cid[0, 0, c] * BLK, -COLS)
        select[pl.ds(c * BLK, BLK), 0:COLS] = onehot(sub + offset == lane)
    loads[3].wait()
    natural = dot(h_ref[...], select[:, 0:COLS])
    for r in range(RT):
        part = natural[r * BLK:(r + 1) * BLK] * jnp.where(r < live_rows, 1.0, 0.0)
        tiles[z, pl.ds(pl.multiple_of(k * ROWS + r * BLK, BLK), BLK), :] = part.astype(jnp.bfloat16)
    pl.semaphore_wait(barrier, len(peers))

    def piece(kk, m, part):
        return tiles.at[m, pl.ds(pl.multiple_of(kk * ROWS + part * PART, PART), PART), :]

    def copy(kind, kk, m, part, row, col):
        return pltpu.make_async_remote_copy(
            src_ref=piece(kk, m, part), dst_ref=piece(kk, m, part),
            send_sem=send.at[kind, m, part], recv_sem=recv.at[kk, m, part],
            device_id={"row": row, "col": col}, device_id_type=MESH_IDS,
        )

    def row_ids_copy(n, owner, row):
        return pltpu.make_async_remote_copy(
            src_ref=meta.at[z, owner], dst_ref=meta.at[z, owner],
            send_sem=meta_send.at[n], recv_sem=meta_recv.at[0, owner],
            device_id={"row": row, "col": z}, device_id_type=MESH_IDS,
        )

    def line_ids_copy(n, owner, col):
        return pltpu.make_async_remote_copy(
            src_ref=meta.at[owner], dst_ref=meta.at[owner],
            send_sem=meta_send.at[n], recv_sem=meta_recv.at[1, owner],
            device_id={"row": k, "col": col}, device_id_type=MESH_IDS,
        )

    def line_copies(m, part, act):
        @pl.when((m <= z) & (z < LINE - 1))
        def _():
            act(copy(0, k, m, part, k, z + 1))

        @pl.when((m >= z) & (z > 0))
        def _():
            act(copy(1, k, m, part, k, z - 1))

        act(copy(2, k, m, part, kx, z))
        act(copy(3, k, m, part, ks, z))

    def start(c):
        c.start()

    def finish(c):
        c.wait_send()

    def arrived(kk, m, part):
        copy(0, kk, m, part, ks, z).wait_recv()

    high = z // 2
    near = z * (1 - high) + (LINE - 1 - z) * high

    def panel_at(t):
        later = t // 2
        m = 2 * later + (t + near * (1 - later)) % 2
        return m * (1 - high) + (LINE - 1 - m) * high

    for n, (row, _) in enumerate(peers[:3]):
        row_ids_copy(n, k, row).start()
    for part in range(PARTS):
        line_copies(z, part, start)
    for row, _ in peers[:3]:
        row_ids_copy(0, row, row).wait_recv()
    for n, (_, col) in enumerate(peers[3:]):
        line_ids_copy(3 + n, z, col).start()
    for _, col in peers[3:]:
        line_ids_copy(3, col, col).wait_recv()
    for m in range(LINE):
        for kk in range(LINE):
            short_ids[pl.ds(m * LINE + kk, 1), :] = meta[m, kk, 6:7, :]
    spell = pltpu.make_async_copy(short_ids, ids, load.at[4])
    spell.start()
    spell.wait()

    def lane_ids(kk, m):
        return jnp.concatenate([meta[m, kk, 0:1, :], meta[m, kk, 1:2, :]], axis=1)

    def natural_mask(kk, m):
        return jnp.concatenate([meta[m, kk, 2 + q:3 + q, :] for q in range(4)], axis=1).astype(jnp.float32)

    def pick_rows(kk, to, of, block_at):
        blocks = []
        for r in range(RT):
            want = ids[to * LINE + kk, r]
            block = jnp.zeros((BLK, ROWS), jnp.bfloat16)
            for a in range(RT):
                same = (ids[of * LINE + kk, a] == want) & (want >= 0)
                block = jnp.where(same, block_at(a), block)
            blocks.append(block)
        return jnp.concatenate(blocks, axis=0)

    sub_wide = lax.broadcasted_iota(jnp.int32, (COLS, ROWS), 0)

    def col_select(m, to):
        return onehot(sub_wide == lane_ids(m, to))

    def wide_slice(index):
        return pl.ds(pl.multiple_of(index * ROWS, ROWS), ROWS)

    def stage(t, carry):
        for now, then in ((0, 1), (0, 2), (1, 3)):
            @pl.when(t == now)
            def _(then=then):
                m1 = panel_at(then)
                for part in range(PARTS):
                    arrived(k, m1, part)
                    line_copies(m1, part, start)

        m = panel_at(t)
        for part in range(PARTS):
            arrived(kx, m, part)
            copy(4, kx, m, part, ks, z).start()
        for to in range(LINE):
            select[:, pl.ds(to * ROWS, ROWS)] = col_select(m, to)
        for part in range(PARTS):
            arrived(ks, m, part)
            arrived(kxs, m, part)

        mask = jnp.concatenate(
            [natural_mask(kk, m) for kk in range(LINE)] + [jnp.zeros((12, COLS), jnp.float32)], axis=0
        )
        masks[m] = dot(mask.astype(jnp.bfloat16), select[:, wide_slice(z)])
        def rows_of(kk, carry):
            wide[...] = dot(tiles[m, wide_slice(kk), :], select[...]).astype(jnp.bfloat16)
            right[m, wide_slice(kk), :] = wide[:, wide_slice(z)]
            for to in range(LINE):
                left[to, wide_slice(kk), wide_slice(m)] = pick_rows(
                    kk, to, m, lambda a, to=to: wide[pl.ds(a * BLK, BLK), pl.ds(to * ROWS, ROWS)]
                )
            return carry

        lax.fori_loop(0, LINE, rows_of, 0)
        values = tiles[m].astype(jnp.float32)
        return carry + jnp.sum(values * values, axis=0, keepdims=True)

    total = lax.fori_loop(0, LINE, stage, jnp.zeros((1, COLS), jnp.float32))

    total = jnp.sum(total, axis=1, keepdims=True)
    count = jnp.int32(0)
    for a in range(LINE):
        for b in range(LINE):
            count += ids[a * LINE + b, RT]
    count = jnp.full((1, 1), count * BLK, jnp.int32).astype(jnp.float32)
    scale = 2.0 * jnp.sqrt(LINE * total / count + 1e-06)
    lin = 1.5 / scale
    cub = 0.5 / scale / scale / scale

    def spread(rows):
        return jnp.concatenate([jnp.broadcast_to(row, (ROWS, row.shape[1])) for row in rows], axis=0)

    def other(d, carry):
        m = (z + d) % LINE
        mask = spread([masks[m, kk:kk + 1, :] for kk in range(LINE)])
        half[...] = (dot(left[m], right[m]) * mask).astype(jnp.bfloat16)
        part = dot(left[m], half[...]) * mask
        picked[0:FULL, :] = (lin * right[m].astype(jnp.float32) - cub * part).astype(jnp.bfloat16)
        for kk in range(LINE):
            left2[pl.ds(kk * ROWS, ROWS), wide_slice(m)] = pick_rows(
                kk, z, m, lambda a, kk=kk: picked[pl.ds(kk * ROWS + a * BLK, BLK), :]
            )
        return carry

    lax.fori_loop(1, LINE, other, 0)

    mask = spread([natural_mask(kk, z) for kk in range(LINE)])
    square2[...] = (dot(left[z], tiles[z]) * mask).astype(jnp.bfloat16)
    select[:, 0:ROWS] = col_select(z, z)
    part = dot(left[z], square2[...]) * mask
    whole[...] = (lin * tiles[z].astype(jnp.float32) - cub * part).astype(jnp.bfloat16)
    left2[:, wide_slice(z)] = dot(whole[...], select[:, 0:ROWS]).astype(jnp.bfloat16)
    square2[...] = (dot(left2[...], whole[...]) * mask).astype(jnp.bfloat16)
    cube = dot(left2[wide_slice(k), :], square2[...]) * natural_mask(k, z)
    update = 1.5 * whole[wide_slice(k), :].astype(jnp.float32) - 0.5 * cube
    final = (update * scale).astype(jnp.bfloat16)
    back = onehot(lax.broadcasted_iota(jnp.int32, (COLS, COLS), 0) == col_full)
    o_ref[...] = dot(final, back).astype(jnp.bfloat16)

    for n, (row, _) in enumerate(peers[:3]):
        row_ids_copy(n, k, row).wait_send()
    for n, (_, col) in enumerate(peers[3:]):
        line_ids_copy(3 + n, z, col).wait_send()

    def drain(m, carry):
        for part in range(PARTS):
            line_copies(m, part, finish)
            copy(4, kx, m, part, ks, z).wait_send()
        return carry

    lax.fori_loop(0, LINE, drain, 0)


def line_shards(hamiltonian, row_ids, col_ids, counts):
    hbm = pl.BlockSpec(memory_space=pl.ANY)
    vmem = pl.BlockSpec(memory_space=pltpu.VMEM)
    bf16, f32 = jnp.bfloat16, jnp.float32
    return pl.pallas_call(
        lines_kernel,
        out_shape=jax.ShapeDtypeStruct((ROWS, COLS), bf16),
        in_specs=[hbm, hbm, hbm, hbm],
        out_specs=vmem,
        scratch_shapes=[
            pltpu.VMEM((ROWS, COLS), bf16),
            pltpu.SMEM(row_ids.shape, jnp.int32),
            pltpu.SMEM(col_ids.shape, jnp.int32),
            pltpu.SMEM(counts.shape, jnp.int32),
            pltpu.VMEM((LINE, FULL, COLS), bf16),
            pltpu.VMEM((LINE, LINE, 8, 128), jnp.int32),
            pltpu.VMEM((LINE * LINE, 128), jnp.int32),
            pltpu.SMEM((LINE * LINE, 128), jnp.int32),
            pltpu.VMEM((LINE, FULL, FULL), bf16),
            pltpu.VMEM((LINE, FULL, ROWS), bf16),
            pltpu.VMEM((ROWS, FULL), bf16),
            pltpu.VMEM((FULL, ROWS), bf16),
            pltpu.VMEM((COLS, FULL), bf16),
            pltpu.VMEM((LINE, 16, ROWS), f32),
            pltpu.VMEM((FULL, ROWS), bf16),
            pltpu.VMEM((FULL, COLS), bf16),
            pltpu.VMEM((FULL, FULL), bf16),
            pltpu.VMEM((FULL, COLS), bf16),
            pltpu.SemaphoreType.DMA((5, LINE, PARTS)),
            pltpu.SemaphoreType.DMA((LINE, LINE, PARTS)),
            pltpu.SemaphoreType.DMA((6,)),
            pltpu.SemaphoreType.DMA((2, LINE)),
            pltpu.SemaphoreType.DMA((5,)),
        ],
        compiler_params=pltpu.CompilerParams(
            collective_id=0, has_side_effects=True, vmem_limit_bytes=48 * 1024 * 1024
        ),
        cost_estimate=pl.CostEstimate(flops=13_000_000_000, bytes_accessed=8_000_000, transcendentals=0),
    )(hamiltonian, row_ids, col_ids, counts)


def shards(hamiltonian, row_ids, col_ids, counts):
    grid_rows = lax.axis_size("row")
    grid_cols = lax.axis_size("col")
    sub_panels = grid_rows // grid_cols
    my_row = lax.axis_index("row")
    my_col = lax.axis_index("col")
    tile_rows = hamiltonian.shape[0]
    tile_cols = hamiltonian.shape[1]
    every_rows, every_cols, every_counts = (
        lax.all_gather(row_ids, ("row", "col"), axis=0, tiled=True),
        lax.all_gather(col_ids, ("row", "col"), axis=0, tiled=True),
        lax.all_gather(counts, ("row", "col"), axis=0, tiled=True),
    )
    every_rows = every_rows.reshape(grid_rows, grid_cols, RT)
    every_cols = every_cols.reshape(grid_rows, grid_cols, CT)
    every_counts = every_counts.reshape(grid_rows, grid_cols, 2)
    row_live = jnp.arange(RT)[None, None, :] < every_counts[:, :, 0:1]
    col_live = jnp.arange(CT)[None, None, :] < every_counts[:, :, 1:2]
    global_rows = jnp.arange(grid_rows, dtype=jnp.int32)[:, None, None] * ACT + every_rows
    global_cols = (
        jnp.arange(grid_cols, dtype=jnp.int32)[None, :, None] * (sub_panels * ACT) + every_cols
    )
    own_rows = every_rows[my_row, my_col]
    own_cols = every_cols[my_row, my_col]
    own_row_live = row_live[my_row, my_col]
    own_col_live = col_live[my_row, my_col]
    block_mask = (
        jnp.repeat(own_row_live, BLK)[:, None] & jnp.repeat(own_col_live, BLK)[None, :]
    ).astype(jnp.float32)
    energy = hamiltonian.astype(jnp.float32) * block_mask
    total = lax.psum(jnp.sum(energy * energy), ("row", "col"))
    live_total = BLK * jnp.sum(every_counts[:, :, 0]).astype(jnp.float32)
    scale = 2.0 * jnp.sqrt(grid_cols * total / live_total + 1e-06)
    current = (energy / scale).astype(jnp.bfloat16)
    panel_rows = every_rows[my_row]
    row_match = (
        (panel_rows[:, None, :] == own_rows[None, :, None])
        & row_live[my_row][:, None, :]
        & own_row_live[None, :, None]
    )
    row_select = row_match.astype(jnp.bfloat16)
    pair_tile = jnp.arange(grid_rows, dtype=jnp.int32) // sub_panels
    left_cols = global_cols[my_row][pair_tile]
    left_live = col_live[my_row][pair_tile]
    right_rows = global_rows[:, my_col]
    right_live = row_live[:, my_col]
    matches = (
        (left_cols[:, None, :] == right_rows[:, :, None])
        & left_live[:, None, :]
        & right_live[:, :, None]
    )
    present_pairs = jnp.sum(matches.astype(jnp.int32), axis=2).reshape(-1)
    column_slot = (
        jnp.sum(jnp.where(matches, jnp.arange(CT, dtype=jnp.int32)[None, None, :], 0), axis=2)
        + pair_tile[:, None] * CT
    ).reshape(-1)
    col_match = (
        (every_cols[:, my_col][:, :, None] == own_cols[None, None, :])
        & col_live[:, my_col][:, :, None]
        & own_col_live[None, None, :]
    )
    col_tiles = col_match.astype(jnp.bfloat16)

    def multiply(left_full, right):
        left_blocks = left_full.reshape(tile_rows, grid_cols * CT, BLK)
        piece = lax.all_gather(right, "row", axis=0, tiled=True)
        piece_rows = piece.shape[0]
        tiles = piece_rows // tile_rows
        tile_index = jnp.arange(tiles, dtype=jnp.int32)
        selector = jnp.take(col_tiles, tile_index, axis=0)
        blocks = piece.reshape(tiles, tile_rows, CT, BLK)
        moved = jnp.einsum("tnxw,txc->tncw", blocks, selector, preferred_element_type=jnp.float32)
        moved = moved.astype(jnp.bfloat16).reshape(piece_rows, tile_cols)
        picked = jnp.take(left_blocks, column_slot, axis=1)
        picked = jnp.where(present_pairs[None, :, None] > 0, picked, jnp.zeros_like(picked))
        picked = picked.reshape(tile_rows, piece_rows)
        return jnp.dot(picked, moved, preferred_element_type=jnp.float32)

    final = None
    for sweep in range(NS_STEPS):
        arrange_blocks = lax.all_gather(current, "col", axis=1, tiled=True).reshape(
            RT, BLK, grid_cols, tile_cols
        )
        mapped = jnp.einsum(
            "mca,axmw->cxmw", row_select, arrange_blocks, preferred_element_type=jnp.float32
        )
        left_full = mapped.astype(jnp.bfloat16).reshape(tile_rows, grid_cols * tile_cols)
        square = multiply(left_full, current).astype(jnp.bfloat16)
        cube = multiply(left_full, square)
        update = 1.5 * current.astype(jnp.float32) - 0.5 * cube
        if sweep + 1 < NS_STEPS:
            current = update.astype(jnp.bfloat16)
        else:
            final = (update * scale).astype(jnp.bfloat16)
    return final


def solution(mesh):
    in_specs = (
        P(("sys", "row"), "col"),
        P(("sys", "row"), "col", None),
        P(("sys", "row"), "col", None),
        P(("sys", "row"), "col", None),
    )
    out_specs = P(("sys", "row"), "col")
    small = mesh.shape["row"] == LINE and mesh.shape["col"] == LINE
    return jax.shard_map(line_shards if small else shards, mesh=mesh, in_specs=in_specs, out_specs=out_specs, check_vma=False)
```
